32 devices in a mesh: front: 8 (over z, core), tile: 4 (over y, x).
Axes of the slice: x: 2, y: 2, z: 4, core: 2. Of those that a mesh axis runs over, the one named last changes fastest.
Arguments:
- pieces: bfloat16 [2304, 256, 128], P(('front', 'tile')), may hold values from -1.59375 to 1.59375
- dest_front: int32 [2304, 1], P(('front', 'tile')), may hold values from 0 to 7; in each aligned block of 72 rows (0 to 71, 72 to 143, ...) at most 9 rows name the same one
- dest_slot: int32 [2304], P(('front', 'tile')), may hold values from 0 to 3
- parent_u: bfloat16 [2048, 1024], P('front', 'tile'), may hold values from -1.59375 to 1.59375
- parent_v: bfloat16 [2048, 1024], P('front', 'tile'), may hold values from -1.59375 to 1.59375
- sketch: bfloat16 [256, 64], replicated, may hold values from -6 to 6
- pivot_inverse: bfloat16 [2048, 256], P('front'), may hold values from -0.01171875 to 0.01171875
Outputs:
- coeff: bfloat16 [2048, 1024], P('front', 'tile')
- cores: float32 [8192, 1024], P(('front', 'tile'))
The draws below stay inside these ranges and needn't reach their ends.
Inputs may be any that keep to these rules, and one draw needn't show every extreme that they name: `dest_front`: among the 72 rows of one device at most 9 name any one front, a bound that some block reaches.
All inputs are finite; a program needn't handle non-finite values.
Results may differ from the reference program's by a relative error of at most 0.017.
Values may be sent and summed in bfloat16 or wider, within the bound.
A program may use at most 128 MiB of HBM per device.

```python
import math
import jax
import jax.numpy as jnp
import numpy as np
from jax import lax

B = 256
R = 64
TILES_DEV = 4
PIECES = 72
CAP = 9
TILES = 16
N_FRONT = 8
N_TILE = 4


def set_ends(drawn, key, smallest, high):
    longest = drawn.shape.index(max(drawn.shape))
    spots = []
    for shift in (0, 1):
        where = [jax.random.randint(jax.random.fold_in(key, axis), (), 0, length) for axis, length in enumerate(drawn.shape)]
        where[longest] = (where[longest] + shift) % drawn.shape[longest]
        spots.append(tuple(where))
    return drawn.at[spots[0]].set(smallest).at[spots[1]].set(high)


def block_scale(key, extent, cuts, low, largest):
    loudness, own = 1.0, jax.random.fold_in(key, 6)
    for dim, blocks in cuts:
        heights = jnp.exp(jax.random.uniform(jax.random.fold_in(own, dim), (blocks,), jnp.float32, low / len(cuts), largest / len(cuts)))
        loudness = loudness * jnp.repeat(heights, extent[dim] // blocks).reshape([-1 if axis == dim else 1 for axis in range(len(extent))])
    return loudness


def deal_out(rng, own, number, rows, count, top, reach, lean):
    order = jax.random.permutation(rng, count)
    heavy_load, common = shares(count, rows * top, reach, lean, True), shares(count, rows * top, reach, lean, False)
    places = jnp.arange(count)

    def named(sizes, rotation):
        used = int((sizes > 0).sum())
        fixed = max(1, used // 4)
        shifted = fixed + (places - fixed + rotation * (used - fixed)) % max(1, count - fixed)
        return jnp.zeros((count,), jnp.int32).at[order[jnp.where(places < fixed, places, shifted)]].set(jnp.asarray(sizes, jnp.int32))

    sizes = jnp.where(number % 4 == 0, named(heavy_load, number // 4), named(common, number - number // 4 - 1))
    mixed = jax.random.permutation(jax.random.fold_in(own, 3), count)
    donor, sink = mixed[0:count // 2 * 2:2], mixed[1:count // 2 * 2:2]
    margin = jnp.minimum(sizes[donor] - 1, reach - sizes[sink]) // 2
    margin = jnp.where((donor == order[0]) | (sink == order[0]) | (sizes[sink] == 0), 0, jnp.maximum(margin, 0))
    shifted = jax.random.randint(jax.random.fold_in(own, 4), (count // 2,), 0, 1 << 20) % (margin + 1)
    sizes = sizes.at[donor].add(-shifted).at[sink].add(shifted)
    members = jnp.searchsorted(jnp.cumsum(sizes), jnp.arange(rows * top), side="right").astype(jnp.int32)
    listing = members.reshape(top, rows).T
    listing = listing[jax.random.permutation(jax.random.fold_in(own, 1), rows)]
    rotation = jax.random.randint(jax.random.fold_in(own, 2), (rows, 1), 0, top)
    return jnp.take_along_axis(listing, (jnp.arange(top)[None, :] + rotation) % top, axis=1)


def shares(number_of, total, reach, slope, full):
    weights = [(1 << 20) // math.isqrt(grade ** slope) + 1 for grade in range(1, number_of + 1)]
    largest = reach if full else min(reach, max(-(-total // number_of), total * weights[0] // sum(weights)))
    least = 1 if total - largest >= number_of - 1 else 0
    counts, rest = [largest] + [least] * (number_of - 1), total - largest - least * (number_of - 1)
    while rest > 0:
        candidates = [i for i in range(1, number_of) if counts[i] < largest] or [i for i in range(1, number_of) if counts[i] < reach]
        mass, budget = sum([weights[i] for i in candidates]), rest
        for i in candidates:
            more = min(reach - counts[i], max(1, budget * weights[i] // mass), rest)
            counts[i] = counts[i] + more
            rest = rest - more
    return np.array(counts)


def gaussian(rng, dims, deviation, bound, cuts=(), kind=jnp.bfloat16):
    values = jax.random.normal(rng, dims, jnp.float32) * deviation
    if len(cuts) > 0:
        values = block_scale(rng, dims, cuts, -0.22, 0.18) * values
    return jnp.clip(values, min=-bound, max=bound).astype(kind)


def setup_inputs(seed: int = 0) -> dict:
    key_of = jax.random.split(jax.random.key(seed), 8)
    pieces = gaussian(key_of[0], (N_FRONT * N_TILE * PIECES, B, 2 * R), 0.2, 1.59375, ((0, 32),))
    dest_front_keys = jax.random.split(jax.random.fold_in(key_of[1], 1), (N_FRONT * N_TILE * PIECES) // PIECES)
    dest_front_turns = jax.random.permutation(jax.random.fold_in(key_of[1], 3), (N_FRONT * N_TILE * PIECES) // PIECES)
    dest_front = jax.vmap(lambda own, number: deal_out(jax.random.fold_in(key_of[1], 2), own, number, PIECES, N_FRONT, 1, CAP, 2))(dest_front_keys, dest_front_turns).reshape((N_FRONT * N_TILE * PIECES, 1))
    dest_slot = set_ends(jax.random.randint(key_of[2], (N_FRONT * N_TILE * PIECES,), 0, TILES_DEV), jax.random.fold_in(key_of[2], 1), 0, TILES_DEV - 1).astype(jnp.int32)
    parent_u = gaussian(key_of[3], (N_FRONT * B, TILES * R), 0.2, 1.59375, ((0, 8), (1, 4)))
    parent_v = gaussian(key_of[4], (N_FRONT * B, TILES * R), 0.2, 1.59375, ((0, 8), (1, 4)))
    sketch = gaussian(key_of[5], (B, R), 1.0, 6.0)
    pivot_inverse = gaussian(key_of[6], (N_FRONT * B, B), (4 * B * B) ** -0.5, 0.01171875, ((0, 8),))
    return {"pieces": pieces, "dest_front": dest_front, "dest_slot": dest_slot, "parent_u": parent_u, "parent_v": parent_v, "sketch": sketch, "pivot_inverse": pivot_inverse}


def rounded(field_values):
    return lax.optimization_barrier(field_values.astype(jnp.bfloat16)).astype(jnp.float32)

def orthonormal_basis(block_unit):
    gram_matrix = jnp.einsum('naj,nav->njv', block_unit, block_unit, precision=lax.Precision.HIGHEST)
    lower = jnp.linalg.cholesky(gram_matrix)
    solved = jax.scipy.linalg.solve_triangular(lower, jnp.swapaxes(block_unit, 1, 2), lower=True)
    return jnp.swapaxes(solved, 1, 2)

def reference(pieces, dest_front, dest_slot, parent_u, parent_v, sketch, pivot_inverse):
    tile_total = N_TILE * TILES_DEV
    tile_count = N_FRONT * tile_total
    row_ids = jnp.arange(N_FRONT * N_TILE * PIECES, dtype=jnp.int32)
    source_tile = row_ids // PIECES % N_TILE
    target_block = (dest_front[:, 0] * tile_total + source_tile * TILES_DEV + dest_slot).astype(jnp.int32)
    blocks = pieces.reshape(N_FRONT * N_TILE, PIECES, B, 2 * R)
    targets = target_block.reshape(N_FRONT * N_TILE, PIECES)

    def tile_major(field_values):
        return field_values.reshape(N_FRONT, B, tile_total, R).transpose(0, 2, 1, 3).reshape(tile_count, B, R).astype(jnp.float32)

    def front_major(field_values):
        return field_values.reshape(N_FRONT, tile_total, B, R).transpose(0, 2, 1, 3).reshape(N_FRONT * B, tile_total * R)
    owned_left_rows = tile_major(parent_u)
    own_right = tile_major(parent_v)
    sketch_full = sketch.astype(jnp.float32)

    def accumulate(term):

        def advance(running, block_unit):
            group, where = block_unit
            left_rows = group[..., :R].astype(jnp.float32)
            right_rows = group[..., R:].astype(jnp.float32)
            return (running + jax.ops.segment_sum(term(left_rows, right_rows, where), where, num_segments=tile_count), None)
        summed, unused = lax.scan(advance, jnp.zeros((tile_count, B, R), jnp.float32), (blocks, targets))
        return summed

    def expand(factor, small):
        return jnp.einsum('pbr,prk->pbk', factor, small)

    def project(factor, other):
        return rounded(jnp.einsum('pbr,pbk->prk', factor, other))

    def sketch_term(left_rows, right_rows, where):
        return expand(left_rows, rounded(jnp.einsum('pbr,bk->prk', right_rows, sketch_full)))
    y_start = accumulate(sketch_term) + sketch_term(owned_left_rows, own_right, None)
    q_start = rounded(orthonormal_basis(y_start))

    def back_term(left_rows, right_rows, where):
        return expand(right_rows, project(left_rows, q_start[where]))
    tile_ids = jnp.arange(tile_count, dtype=jnp.int32)
    z_mid = rounded(accumulate(back_term) + back_term(owned_left_rows, own_right, tile_ids))

    def forth_term(left_rows, right_rows, where):
        return expand(left_rows, project(right_rows, z_mid[where]))
    y_end = accumulate(forth_term) + forth_term(owned_left_rows, own_right, tile_ids)
    q_end = rounded(orthonormal_basis(y_end))

    def final_term(left_rows, right_rows, where):
        return expand(right_rows, project(left_rows, q_end[where]))
    w_end = accumulate(final_term) + final_term(owned_left_rows, own_right, tile_ids)
    coeff = front_major(w_end).astype(jnp.bfloat16)

    def couple(front_pair):
        block_unit, inverse = front_pair
        pivoted = jnp.dot(inverse.astype(jnp.float32), block_unit.astype(jnp.float32), preferred_element_type=jnp.float32).astype(jnp.bfloat16)
        return jnp.dot(block_unit.T.astype(jnp.float32), pivoted.astype(jnp.float32), preferred_element_type=jnp.float32)
    stacked = lax.map(couple, (coeff.reshape(N_FRONT, B, tile_total * R), pivot_inverse.reshape(N_FRONT, B, B)))
    cores = stacked.reshape(N_FRONT * tile_total * R, tile_total * R)
    return (coeff, cores)
```

```python
import functools

import jax
import jax.numpy as jnp
from jax import lax
from jax.experimental import pallas as pl
from jax.experimental.pallas import tpu as pltpu
from jax.sharding import PartitionSpec as P

B = 256
R = 64
TILES_DEV = 4
CAP = 9
PAIRS = (CAP + 1) // 2
SLOTS = 2 * PAIRS
MESH = pl.DeviceIdType.MESH
F32 = jnp.float32
BF16 = jnp.bfloat16
HIGHEST = lax.Precision.HIGHEST


def dot_nt(a, b, precision=None):
    return lax.dot_general(
        a, b, (((1,), (1,)), ((), ())), precision=precision, preferred_element_type=F32
    )


def dot_nn(a, b, precision=None):
    return lax.dot_general(
        a, b, (((1,), (0,)), ((), ())), precision=precision, preferred_element_type=F32
    )


def merge_kernel(
    chips, table_ref, pieces_ref, pu_ref, pv_ref, out_ref,
    part, ex_out, ex_in, up_out, up_in, dn_out, dn_in,
    ex_send, ex_recv, up_send, up_recv, dn_send, dn_recv,
):
    f = lax.axis_index("front")
    z = lax.div(f, 2)
    c = lax.rem(f, 2)
    sibling = 2 * z + 1 - c
    above = lax.rem(f + 2, 2 * chips)
    below = lax.rem(f + 2 * chips - 2, 2 * chips)
    last = chips - 1

    barrier = pltpu.get_barrier_semaphore()
    pl.semaphore_signal(barrier, inc=1, device_id={"front": sibling}, device_id_type=MESH)

    @pl.when(z > 0)
    def _():
        pl.semaphore_signal(barrier, inc=1, device_id={"front": below}, device_id_type=MESH)

    @pl.when(z < last)
    def _():
        pl.semaphore_signal(barrier, inc=1, device_id={"front": above}, device_id_type=MESH)

    pl.semaphore_wait(barrier, 1 + (z > 0).astype(jnp.int32) + (z < last).astype(jnp.int32))

    def copy(kind, i):
        src, dst, send, recv, peer = {
            "ex": (ex_out, ex_in, ex_send, ex_recv, sibling),
            "up": (up_out, up_in, up_send, up_recv, above),
            "dn": (dn_out, dn_in, dn_send, dn_recv, below),
        }[kind]
        return pltpu.make_async_remote_copy(
            src_ref=src.at[i], dst_ref=dst.at[i], send_sem=send.at[i], recv_sem=recv.at[i],
            device_id={"front": peer}, device_id_type=MESH,
        )

    lane = lax.broadcasted_iota(jnp.int32, (1, 2 * R), 1)

    def partial(e):
        lefts, rights, owners = [], [], []
        for pair in range(PAIRS):
            first = table_ref[e * SLOTS + 2 * pair]
            second = table_ref[e * SLOTS + 2 * pair + 1]
            a = pieces_ref[lax.div(first, 8)]
            b = pieces_ref[lax.div(second, 8)]
            lefts.append(jnp.concatenate((a[:, :R], b[:, :R]), axis=1))
            rights.append(jnp.concatenate((a[:, R:], b[:, R:]), axis=1))
            owners.append(jnp.where(lane < R, lax.rem(first, 8), lax.rem(second, 8)))
        left = jnp.concatenate(lefts, axis=1)
        right = jnp.concatenate(rights, axis=1)
        owner = jnp.concatenate(owners, axis=1)
        sums = []
        for s in range(TILES_DEV):
            mask = jnp.where(owner == s, 1.0, 0.0).astype(BF16)
            sums.append(dot_nt(left * mask, right))
        return sums

    def flow(kind, t, s, incoming):
        i = t * TILES_DEV + s
        copy("ex", i).wait_recv()
        total = part[i] + ex_in[i].astype(F32)
        out = up_out if kind == "up" else dn_out
        if incoming:
            copy(kind, i).wait_recv()
            total = total + (up_in if kind == "up" else dn_in)[i].astype(F32)
        out[i] = total.astype(BF16)
        copy(kind, i).start()

    def end_flows(k):
        @pl.when(z == 0)
        def _():
            lax.fori_loop(0, TILES_DEV, lambda s, _: flow("up", last - k, s, False), None)

        @pl.when(z == last)
        def _():
            lax.fori_loop(0, TILES_DEV, lambda s, _: flow("dn", k, s, False), None)

    def compute(k, _):
        t = jnp.where(2 * z < chips, last - k, k)
        for s, total in enumerate(partial(2 * t + 1 - c)):
            ex_out[t * TILES_DEV + s] = total.astype(BF16)
            copy("ex", t * TILES_DEV + s).start()
        for s, total in enumerate(partial(2 * t + c)):
            part[t * TILES_DEV + s] = total

        @pl.when(k > 0)
        def _():
            end_flows(k - 1)

    lax.fori_loop(0, chips, compute, None)

    for s in range(TILES_DEV):
        cols = slice(s * R, (s + 1) * R)
        part[z * TILES_DEV + s] += dot_nt(pu_ref[:, cols], pv_ref[:, cols])

    def tick(n, _):
        up_n = n - z
        dn_n = n - (last - z)

        @pl.when((up_n >= 0) & (up_n < TILES_DEV * (last - z)))
        def _():
            flow("up", last - lax.div(up_n, TILES_DEV), lax.rem(up_n, TILES_DEV), True)

        @pl.when((dn_n >= 0) & (dn_n < TILES_DEV * z))
        def _():
            flow("dn", lax.div(dn_n, TILES_DEV), lax.rem(dn_n, TILES_DEV), True)

    @pl.when((z > 0) & (z < last))
    def _():
        lax.fori_loop(0, TILES_DEV * last + last, tick, None)

    def finish(s, _):
        i = z * TILES_DEV + s
        copy("ex", i).wait_recv()
        part[i] += ex_in[i].astype(F32)

        @pl.when(z > 0)
        def _():
            copy("up", i).wait_recv()
            part[i] += up_in[i].astype(F32)

        @pl.when(z < last)
        def _():
            copy("dn", i).wait_recv()
            part[i] += dn_in[i].astype(F32)

        out_ref[s] = part[i].astype(BF16)

    lax.fori_loop(0, TILES_DEV, finish, None)

    def drain(i, _):
        copy("ex", i).wait_send()

        @pl.when(i >= TILES_DEV * (z + 1))
        def _():
            copy("up", i).wait_send()

        @pl.when(i < TILES_DEV * z)
        def _():
            copy("dn", i).wait_send()

    lax.fori_loop(0, TILES_DEV * chips, drain, None)


def merge(table, pieces, parent_u, parent_v):
    fronts = lax.axis_size("front")
    chips = fronts // 2
    chunks = chips * TILES_DEV
    tile = (chunks, B, B)
    return pl.pallas_call(
        functools.partial(merge_kernel, chips),
        out_shape=jax.ShapeDtypeStruct((TILES_DEV, B, B), BF16),
        in_specs=[pl.BlockSpec(memory_space=pltpu.SMEM)]
        + [pl.BlockSpec(memory_space=pltpu.VMEM)] * 3,
        out_specs=pl.BlockSpec(memory_space=pltpu.VMEM),
        scratch_shapes=[pltpu.VMEM(tile, F32)]
        + [pltpu.VMEM(tile, BF16)] * 6
        + [pltpu.SemaphoreType.DMA((chunks,))] * 6,
        compiler_params=pltpu.CompilerParams(
            collective_id=0, has_side_effects=True, vmem_limit_bytes=56 * 2**20
        ),
        name="merge",
    )(table, pieces, parent_u, parent_v)


def basis(y, work):
    eye = (
        lax.broadcasted_iota(jnp.int32, (R, R), 0) == lax.broadcasted_iota(jnp.int32, (R, R), 1)
    ).astype(F32)
    for t in range(TILES_DEV):
        gram = dot_nt(y[t], y[t], HIGHEST)
        work[:, t, :] = jnp.concatenate((gram, eye), axis=1)
    rows = [work[i] for i in range(R)]
    for j in range(R):
        row = rows[j]
        pivot = jnp.broadcast_to(row[:, j : j + 1], row.shape)
        scaled = row * (1.0 / pivot)
        for i in range(j + 1, R):
            rows[i] = rows[i] - row[:, i : i + 1] * scaled
        work[j] = row * lax.rsqrt(pivot)
    return [
        dot_nn(work[:, t, :][:, R:], y[t], HIGHEST).astype(BF16) for t in range(TILES_DEV)
    ]


def compress_kernel(m_ref, sketch_ref, pivot_ref, w_ref, coeff_ref, pivoted_ref, work):
    tiles = range(TILES_DEV)
    work[...] = jnp.ones_like(work)
    sketch_t = sketch_ref[...].T
    y = [dot_nt(sketch_t, m_ref[t]) for t in tiles]
    q = basis(y, work)
    mid = [dot_nn(q[t], m_ref[t]).astype(BF16) for t in tiles]
    y = [dot_nt(mid[t], m_ref[t]) for t in tiles]
    q = basis(y, work)
    w = jnp.concatenate([dot_nn(q[t], m_ref[t]) for t in tiles], axis=0)
    w_half = w.astype(BF16)
    w_ref[...] = w_half
    pivoted_ref[...] = dot_nt(w_half, pivot_ref[...]).astype(BF16)
    coeff_ref[...] = w.T.astype(BF16)


def compress(merged, sketch, pivot_inverse):
    wide = TILES_DEV * R
    return pl.pallas_call(
        compress_kernel,
        out_shape=(
            jax.ShapeDtypeStruct((wide, B), BF16),
            jax.ShapeDtypeStruct((B, wide), BF16),
            jax.ShapeDtypeStruct((wide, B), BF16),
        ),
        in_specs=[pl.BlockSpec(memory_space=pltpu.VMEM)] * 3,
        out_specs=[pl.BlockSpec(memory_space=pltpu.VMEM)] * 3,
        scratch_shapes=[pltpu.VMEM((R, 8, 2 * R), F32)],
        compiler_params=pltpu.CompilerParams(vmem_limit_bytes=32 * 2**20),
        name="compress",
    )(merged, sketch, pivot_inverse)


def couple_kernel(ranks, w_ref, p_ref, cores_ref, gathered, send, recv):
    me = lax.axis_index("tile")
    barrier = pltpu.get_barrier_semaphore()
    for d in range(1, ranks):
        peer = lax.rem(me + d, ranks)
        pl.semaphore_signal(barrier, inc=1, device_id={"tile": peer}, device_id_type=MESH)
    pl.semaphore_wait(barrier, ranks - 1)

    def copy(d):
        return pltpu.make_async_remote_copy(
            src_ref=p_ref, dst_ref=gathered.at[d - 1], send_sem=send.at[d - 1],
            recv_sem=recv.at[d - 1], device_id={"tile": lax.rem(me + d, ranks)},
            device_id_type=MESH,
        )

    for d in range(1, ranks):
        copy(d).start()
    wide = TILES_DEV * R

    def place(source, block):
        cores_ref[:, pl.ds(pl.multiple_of(source * wide, wide), wide)] = dot_nt(w_ref[...], block)

    place(me, p_ref[...])
    for d in range(1, ranks):
        copy(d).wait_recv()
        place(lax.rem(me + ranks - d, ranks), gathered[d - 1])
    for d in range(1, ranks):
        copy(d).wait_send()


def couple(w, pivoted):
    ranks = lax.axis_size("tile")
    wide = TILES_DEV * R
    return pl.pallas_call(
        functools.partial(couple_kernel, ranks),
        out_shape=jax.ShapeDtypeStruct((wide, ranks * wide), F32),
        in_specs=[pl.BlockSpec(memory_space=pltpu.VMEM)] * 2,
        out_specs=pl.BlockSpec(memory_space=pltpu.VMEM),
        scratch_shapes=[
            pltpu.VMEM((ranks - 1, wide, B), BF16),
            pltpu.SemaphoreType.DMA((ranks - 1,)),
            pltpu.SemaphoreType.DMA((ranks - 1,)),
        ],
        compiler_params=pltpu.CompilerParams(
            collective_id=1, has_side_effects=True, vmem_limit_bytes=32 * 2**20
        ),
        name="couple",
    )(w, pivoted)


def shards(pieces, dest_front, dest_slot, parent_u, parent_v, sketch, pivot_inverse):
    fronts = lax.axis_size("front")
    count = pieces.shape[0]
    ids = jnp.arange(count, dtype=jnp.int32)
    front_ids = dest_front[:, 0]
    prior = jnp.sum(
        ((front_ids[:, None] == front_ids[None, :]) & (ids[None, :] < ids[:, None])).astype(
            jnp.int32
        ),
        axis=1,
    )
    places = front_ids * SLOTS + prior
    hit = places[:, None] == jnp.arange(fronts * SLOTS, dtype=jnp.int32)[None, :]
    code = (ids * 8 + dest_slot - TILES_DEV)[:, None]
    table = jnp.sum(jnp.where(hit, code, 0), axis=0) + TILES_DEV
    merged = merge(table, pieces, parent_u, parent_v)
    w, coeff, pivoted = compress(merged, sketch, pivot_inverse)
    return (coeff, couple(w, pivoted))


def solution(mesh):
    return jax.shard_map(
        shards,
        mesh=mesh,
        in_specs=(
            P(("front", "tile"), None, None),
            P(("front", "tile"), None),
            P(("front", "tile")),
            P("front", "tile"),
            P("front", "tile"),
            P(),
            P("front", None),
        ),
        out_specs=(P("front", "tile"), P(("front", "tile"), None)),
        check_vma=False,
    )
```

```python
import functools

import jax
import jax.numpy as jnp
from jax import lax
from jax.experimental import pallas as pl
from jax.experimental.pallas import tpu as pltpu
from jax.sharding import PartitionSpec as P

B = 256
R = 64
TILES_DEV = 4
CAP = 9
PAIRS = (CAP + 1) // 2
SLOTS = 2 * PAIRS
MESH = pl.DeviceIdType.MESH
F32 = jnp.float32
BF16 = jnp.bfloat16
HIGHEST = lax.Precision.HIGHEST


def dot_nt(a, b, precision=None):
    return lax.dot_general(
        a, b, (((1,), (1,)), ((), ())), precision=precision, preferred_element_type=F32
    )


def dot_nn(a, b, precision=None):
    return lax.dot_general(
        a, b, (((1,), (0,)), ((), ())), precision=precision, preferred_element_type=F32
    )


def merge_kernel(
    chips, table_ref, pieces_hbm, pu_ref, pv_ref, out_ref, pieces_ref, load_sem,
    part, ex_out, ex_in, up_out, up_in, dn_out, dn_in,
    ex_send, ex_recv, up_send, up_recv, dn_send, dn_recv,
):
    f = lax.axis_index("front")
    z = lax.div(f, 2)
    c = lax.rem(f, 2)
    sibling = 2 * z + 1 - c
    above = lax.rem(f + 2, 2 * chips)
    below = lax.rem(f + 2 * chips - 2, 2 * chips)
    last = chips - 1

    load = pltpu.make_async_copy(pieces_hbm, pieces_ref, load_sem)
    load.start()
    barrier = pltpu.get_barrier_semaphore()
    pl.semaphore_signal(barrier, inc=1, device_id={"front": sibling}, device_id_type=MESH)

    @pl.when(z > 0)
    def _():
        pl.semaphore_signal(barrier, inc=1, device_id={"front": below}, device_id_type=MESH)

    @pl.when(z < last)
    def _():
        pl.semaphore_signal(barrier, inc=1, device_id={"front": above}, device_id_type=MESH)

    pl.semaphore_wait(barrier, 1 + (z > 0).astype(jnp.int32) + (z < last).astype(jnp.int32))

    load.wait()

    def copy(kind, i):
        src, dst, send, recv, peer = {
            "ex": (ex_out, ex_in, ex_send, ex_recv, sibling),
            "up": (up_out, up_in, up_send, up_recv, above),
            "dn": (dn_out, dn_in, dn_send, dn_recv, below),
        }[kind]
        return pltpu.make_async_remote_copy(
            src_ref=src.at[i], dst_ref=dst.at[i], send_sem=send.at[i], recv_sem=recv.at[i],
            device_id={"front": peer}, device_id_type=MESH,
        )

    lane = lax.broadcasted_iota(jnp.int32, (1, 2 * R), 1)

    def partial(e):
        lefts, rights, owners = [], [], []
        for pair in range(PAIRS):
            first = table_ref[e * SLOTS + 2 * pair]
            second = table_ref[e * SLOTS + 2 * pair + 1]
            a = pieces_ref[lax.div(first, 8)]
            b = pieces_ref[lax.div(second, 8)]
            lefts.append(jnp.concatenate((a[:, :R], b[:, :R]), axis=1))
            rights.append(jnp.concatenate((a[:, R:], b[:, R:]), axis=1))
            owners.append(jnp.where(lane < R, lax.rem(first, 8), lax.rem(second, 8)))
        left = jnp.concatenate(lefts, axis=1)
        right = jnp.concatenate(rights, axis=1)
        owner = jnp.concatenate(owners, axis=1)
        for s in range(TILES_DEV):
            mask = jnp.where(owner == s, 1.0, 0.0).astype(BF16)
            yield dot_nt(left * mask, right)

    def flow(kind, t, s, incoming):
        i = t * TILES_DEV + s
        copy("ex", i).wait_recv()
        total = part[i] + ex_in[i].astype(F32)
        out = up_out if kind == "up" else dn_out
        if incoming:
            copy(kind, i).wait_recv()
            total = total + (up_in if kind == "up" else dn_in)[i].astype(F32)
        out[i] = total.astype(BF16)
        copy(kind, i).start()

    def end_flows(k):
        @pl.when(z == 0)
        def _():
            lax.fori_loop(0, TILES_DEV, lambda s, _: flow("up", last - k, s, False), None)

        @pl.when(z == last)
        def _():
            lax.fori_loop(0, TILES_DEV, lambda s, _: flow("dn", k, s, False), None)

    def compute(k, _):
        t = jnp.where(2 * z < chips, last - k, k)
        for s, total in enumerate(partial(2 * t + 1 - c)):
            ex_out[t * TILES_DEV + s] = total.astype(BF16)
            copy("ex", t * TILES_DEV + s).start()
        for s, total in enumerate(partial(2 * t + c)):
            part[t * TILES_DEV + s] = total

        @pl.when(k < last)
        def _():
            end_flows(k)

    lax.fori_loop(0, chips, compute, None)

    for s in range(TILES_DEV):
        cols = slice(s * R, (s + 1) * R)
        part[z * TILES_DEV + s] += dot_nt(pu_ref[:, cols], pv_ref[:, cols])

    def tick(n, _):
        up_n = n - z
        dn_n = n - (last - z)

        @pl.when((up_n >= 0) & (up_n < TILES_DEV * (last - z)))
        def _():
            flow("up", last - lax.div(up_n, TILES_DEV), lax.rem(up_n, TILES_DEV), True)

        @pl.when((dn_n >= 0) & (dn_n < TILES_DEV * z))
        def _():
            flow("dn", lax.div(dn_n, TILES_DEV), lax.rem(dn_n, TILES_DEV), True)

    @pl.when((z > 0) & (z < last))
    def _():
        lax.fori_loop(0, TILES_DEV * last + last, tick, None)

    def finish(s, _):
        i = z * TILES_DEV + s
        copy("ex", i).wait_recv()
        part[i] += ex_in[i].astype(F32)

        @pl.when(z > 0)
        def _():
            copy("up", i).wait_recv()
            part[i] += up_in[i].astype(F32)

        @pl.when(z < last)
        def _():
            copy("dn", i).wait_recv()
            part[i] += dn_in[i].astype(F32)

        out_ref[s] = part[i].astype(BF16)

    lax.fori_loop(0, TILES_DEV, finish, None)

    def drain(i, _):
        copy("ex", i).wait_send()

        @pl.when(i >= TILES_DEV * (z + 1))
        def _():
            copy("up", i).wait_send()

        @pl.when(i < TILES_DEV * z)
        def _():
            copy("dn", i).wait_send()

    lax.fori_loop(0, TILES_DEV * chips, drain, None)


def merge(table, pieces, parent_u, parent_v):
    fronts = lax.axis_size("front")
    chips = fronts // 2
    chunks = chips * TILES_DEV
    tile = (chunks, B, B)
    return pl.pallas_call(
        functools.partial(merge_kernel, chips),
        out_shape=jax.ShapeDtypeStruct((TILES_DEV, B, B), BF16),
        in_specs=[
            pl.BlockSpec(memory_space=pltpu.SMEM),
            pl.BlockSpec(memory_space=pl.ANY),
            pl.BlockSpec(memory_space=pltpu.VMEM),
            pl.BlockSpec(memory_space=pltpu.VMEM),
        ],
        out_specs=pl.BlockSpec(memory_space=pltpu.VMEM),
        scratch_shapes=[
            pltpu.VMEM(pieces.shape, BF16),
            pltpu.SemaphoreType.DMA,
            pltpu.VMEM(tile, F32),
        ]
        + [pltpu.VMEM(tile, BF16)] * 6
        + [pltpu.SemaphoreType.DMA((chunks,))] * 6,
        compiler_params=pltpu.CompilerParams(
            collective_id=0, has_side_effects=True, vmem_limit_bytes=56 * 2**20
        ),
        name="merge",
    )(table, pieces, parent_u, parent_v)


def basis(y, work):
    eye = (
        lax.broadcasted_iota(jnp.int32, (R, R), 0) == lax.broadcasted_iota(jnp.int32, (R, R), 1)
    ).astype(F32)
    for t in range(TILES_DEV):
        gram = dot_nt(y[t], y[t], HIGHEST)
        work[:, t, :] = jnp.concatenate((gram, eye), axis=1)
    rows = [work[i] for i in range(R)]
    for j in range(R):
        row = rows[j]
        pivot = jnp.broadcast_to(row[:, j : j + 1], row.shape)
        inverse = lax.rsqrt(pivot)
        scaled = row * (inverse * inverse)
        for i in range(j + 1, R):
            rows[i] = rows[i] - row[:, i : i + 1] * scaled
        work[j] = row * inverse
    return [
        dot_nn(work[:, t, :][:, R:], y[t], HIGHEST).astype(BF16) for t in range(TILES_DEV)
    ]


def compress_kernel(m_ref, sketch_ref, pivot_ref, w_ref, coeff_ref, pivoted_ref, work):
    tiles = range(TILES_DEV)
    work[...] = jnp.ones_like(work)
    sketch_t = sketch_ref[...]
    y = [dot_nt(sketch_t, m_ref[t]) for t in tiles]
    q = basis(y, work)
    mid = [dot_nn(q[t], m_ref[t]).astype(BF16) for t in tiles]
    y = [dot_nt(mid[t], m_ref[t]) for t in tiles]
    q = basis(y, work)
    w = jnp.concatenate([dot_nn(q[t], m_ref[t]) for t in tiles], axis=0)
    w_half = w.astype(BF16)
    w_ref[...] = w_half
    pivoted_ref[...] = dot_nt(w_half, pivot_ref[...]).astype(BF16)
    coeff_ref[...] = w.T.astype(BF16)


def compress(merged, sketch, pivot_inverse):
    wide = TILES_DEV * R
    return pl.pallas_call(
        compress_kernel,
        out_shape=(
            jax.ShapeDtypeStruct((wide, B), BF16),
            jax.ShapeDtypeStruct((B, wide), BF16),
            jax.ShapeDtypeStruct((wide, B), BF16),
        ),
        in_specs=[pl.BlockSpec(memory_space=pltpu.VMEM)] * 3,
        out_specs=[pl.BlockSpec(memory_space=pltpu.VMEM)] * 3,
        scratch_shapes=[pltpu.VMEM((R, 8, 2 * R), F32)],
        compiler_params=pltpu.CompilerParams(vmem_limit_bytes=32 * 2**20),
        name="compress",
    )(merged, sketch, pivot_inverse)


def couple_kernel(ranks, w_ref, p_ref, cores_ref, gathered, send, recv):
    me = lax.axis_index("tile")
    barrier = pltpu.get_barrier_semaphore()
    for d in range(1, ranks):
        peer = lax.rem(me + d, ranks)
        pl.semaphore_signal(barrier, inc=1, device_id={"tile": peer}, device_id_type=MESH)
    pl.semaphore_wait(barrier, ranks - 1)

    def copy(d):
        return pltpu.make_async_remote_copy(
            src_ref=p_ref, dst_ref=gathered.at[d - 1], send_sem=send.at[d - 1],
            recv_sem=recv.at[d - 1], device_id={"tile": lax.rem(me + d, ranks)},
            device_id_type=MESH,
        )

    for d in range(1, ranks):
        copy(d).start()
    wide = TILES_DEV * R

    def place(source, block):
        cores_ref[:, pl.ds(pl.multiple_of(source * wide, wide), wide)] = dot_nt(w_ref[...], block)

    place(me, p_ref[...])
    for d in range(1, ranks):
        copy(d).wait_recv()
        place(lax.rem(me + ranks - d, ranks), gathered[d - 1])
    for d in range(1, ranks):
        copy(d).wait_send()


def couple(w, pivoted):
    ranks = lax.axis_size("tile")
    wide = TILES_DEV * R
    return pl.pallas_call(
        functools.partial(couple_kernel, ranks),
        out_shape=jax.ShapeDtypeStruct((wide, ranks * wide), F32),
        in_specs=[pl.BlockSpec(memory_space=pltpu.VMEM)] * 2,
        out_specs=pl.BlockSpec(memory_space=pltpu.VMEM),
        scratch_shapes=[
            pltpu.VMEM((ranks - 1, wide, B), BF16),
            pltpu.SemaphoreType.DMA((ranks - 1,)),
            pltpu.SemaphoreType.DMA((ranks - 1,)),
        ],
        compiler_params=pltpu.CompilerParams(
            collective_id=1, has_side_effects=True, vmem_limit_bytes=32 * 2**20
        ),
        name="couple",
    )(w, pivoted)


def shards(pieces, dest_front, dest_slot, parent_u, parent_v, sketch, pivot_inverse):
    fronts = lax.axis_size("front")
    count = pieces.shape[0]
    ids = jnp.arange(count, dtype=jnp.int32)
    front_ids = dest_front[:, 0]
    prior = jnp.sum(
        ((front_ids[:, None] == front_ids[None, :]) & (ids[None, :] < ids[:, None])).astype(
            jnp.int32
        ),
        axis=1,
    )
    places = front_ids * SLOTS + prior
    hit = places[:, None] == jnp.arange(fronts * SLOTS, dtype=jnp.int32)[None, :]
    code = (ids * 8 + dest_slot - TILES_DEV)[:, None]
    table = jnp.sum(jnp.where(hit, code, 0), axis=0) + TILES_DEV
    merged = merge(table, pieces, parent_u, parent_v)
    w, coeff, pivoted = compress(merged, sketch.T, pivot_inverse)
    return (coeff, couple(w, pivoted))


def solution(mesh):
    return jax.shard_map(
        shards,
        mesh=mesh,
        in_specs=(
            P(("front", "tile"), None, None),
            P(("front", "tile"), None),
            P(("front", "tile")),
            P("front", "tile"),
            P("front", "tile"),
            P(),
            P("front", None),
        ),
        out_specs=(P("front", "tile"), P(("front", "tile"), None)),
        check_vma=False,
    )
```

```python
import functools

import jax
import jax.numpy as jnp
from jax import lax
from jax.experimental import pallas as pl
from jax.experimental.pallas import tpu as pltpu
from jax.sharding import PartitionSpec as P

B = 256
R = 64
TILES_DEV = 4
CAP = 9
PAIRS = (CAP + 1) // 2
SLOTS = 2 * PAIRS
MESH = pl.DeviceIdType.MESH
F32 = jnp.float32
BF16 = jnp.bfloat16
HIGHEST = lax.Precision.HIGHEST


def dot_nt(a, b, precision=None):
    return lax.dot_general(
        a, b, (((1,), (1,)), ((), ())), precision=precision, preferred_element_type=F32
    )


def dot_nn(a, b, precision=None):
    return lax.dot_general(
        a, b, (((1,), (0,)), ((), ())), precision=precision, preferred_element_type=F32
    )


def works_on_pair(z, chips):
    return lax.rem(z, 2) == jnp.where(2 * z < chips, 0, 1)


def targets_ahead(z, chips):
    even = lax.rem(z, 2) == 0
    shift = jnp.where(even, jnp.where(2 * z < chips, -1, 1), 0)
    return chips - 1 - z + shift


def merge_kernel(
    chips, table_ref, pieces_hbm, pu_ref, pv_ref, out_ref, pieces_ref, load_sem,
    part, ex_out, ex_in, up_out, up_in, dn_out, dn_in,
    ex_send, ex_recv, up_send, up_recv, dn_send, dn_recv,
):
    f = lax.axis_index("front")
    z = lax.div(f, 2)
    c = lax.rem(f, 2)
    sibling = 2 * z + 1 - c
    above = lax.rem(f + 2, 2 * chips)
    below = lax.rem(f + 2 * chips - 2, 2 * chips)
    last = chips - 1
    up_count = TILES_DEV * targets_ahead(z, chips)
    dn_count = TILES_DEV * targets_ahead(last - z, chips)

    load = pltpu.make_async_copy(pieces_hbm, pieces_ref, load_sem)
    load.start()
    barrier = pltpu.get_barrier_semaphore()
    pl.semaphore_signal(barrier, inc=1, device_id={"front": sibling}, device_id_type=MESH)

    @pl.when(z > 0)
    def _():
        pl.semaphore_signal(barrier, inc=1, device_id={"front": below}, device_id_type=MESH)

    @pl.when(z < last)
    def _():
        pl.semaphore_signal(barrier, inc=1, device_id={"front": above}, device_id_type=MESH)

    pl.semaphore_wait(barrier, 1 + (z > 0).astype(jnp.int32) + (z < last).astype(jnp.int32))

    load.wait()

    def copy(kind, i):
        src, dst, send, recv, peer = {
            "ex": (ex_out, ex_in, ex_send, ex_recv, sibling),
            "up": (up_out, up_in, up_send, up_recv, above),
            "dn": (dn_out, dn_in, dn_send, dn_recv, below),
        }[kind]
        return pltpu.make_async_remote_copy(
            src_ref=src.at[i], dst_ref=dst.at[i], send_sem=send.at[i], recv_sem=recv.at[i],
            device_id={"front": peer}, device_id_type=MESH,
        )

    lane = lax.broadcasted_iota(jnp.int32, (1, 2 * R), 1)

    def partial(e):
        lefts, rights, owners = [], [], []
        for pair in range(PAIRS):
            first = table_ref[e * SLOTS + 2 * pair]
            second = table_ref[e * SLOTS + 2 * pair + 1]
            a = pieces_ref[lax.div(first, 8)]
            b = pieces_ref[lax.div(second, 8)]
            lefts.append(jnp.concatenate((a[:, :R], b[:, :R]), axis=1))
            rights.append(jnp.concatenate((a[:, R:], b[:, R:]), axis=1))
            owners.append(jnp.where(lane < R, lax.rem(first, 8), lax.rem(second, 8)))
        left = jnp.concatenate(lefts, axis=1)
        right = jnp.concatenate(rights, axis=1)
        owner = jnp.concatenate(owners, axis=1)
        for s in range(TILES_DEV):
            mask = jnp.where(owner == s, 1.0, 0.0).astype(BF16)
            yield dot_nt(left * mask, right)

    def flow(kind, t, s, incoming):
        i = t * TILES_DEV + s
        copy("ex", i).wait_recv()
        total = part[i] + ex_in[i].astype(F32)
        out = up_out if kind == "up" else dn_out
        if incoming:
            copy(kind, i).wait_recv()
            total = total + (up_in if kind == "up" else dn_in)[i].astype(F32)
        out[i] = total.astype(BF16)
        copy(kind, i).start()

    def end_flows(k):
        @pl.when(z == 0)
        def _():
            lax.fori_loop(0, TILES_DEV, lambda s, _: flow("up", last - k, s, False), None)

        @pl.when(z == last)
        def _():
            lax.fori_loop(0, TILES_DEV, lambda s, _: flow("dn", k, s, False), None)

    def compute(k, _):
        t = jnp.where(2 * z < chips, last - k, k)
        for s, total in enumerate(partial(2 * t + 1 - c)):
            ex_out[t * TILES_DEV + s] = total.astype(BF16)
            copy("ex", t * TILES_DEV + s).start()
        for s, total in enumerate(partial(2 * t + c)):
            part[t * TILES_DEV + s] = total

        @pl.when(k < last - 1)
        def _():
            end_flows(k)

    lax.fori_loop(0, chips, compute, None)

    for s in range(TILES_DEV):
        cols = slice(s * R, (s + 1) * R)
        part[z * TILES_DEV + s] += dot_nt(pu_ref[:, cols], pv_ref[:, cols])

    out_ref[...] = jnp.zeros_like(out_ref)

    def tick(n, _):
        up_n = n - z
        dn_n = n - (last - z)

        @pl.when((up_n >= 0) & (up_n < up_count))
        def _():
            flow("up", last - lax.div(up_n, TILES_DEV), lax.rem(up_n, TILES_DEV), True)

        @pl.when((dn_n >= 0) & (dn_n < dn_count))
        def _():
            flow("dn", lax.div(dn_n, TILES_DEV), lax.rem(dn_n, TILES_DEV), True)

    @pl.when((z > 0) & (z < last))
    def _():
        lax.fori_loop(0, TILES_DEV * chips + last, tick, None)

    def finish(n, _):
        place = jnp.where(2 * z < chips, lax.div(n, TILES_DEV), 1 - lax.div(n, TILES_DEV))
        place = place * TILES_DEV + lax.rem(n, TILES_DEV)
        i = (z - lax.rem(z, 2)) * TILES_DEV + place
        copy("ex", i).wait_recv()
        part[i] += ex_in[i].astype(F32)

        @pl.when(z > 0)
        def _():
            copy("up", i).wait_recv()
            part[i] += up_in[i].astype(F32)

        @pl.when(z < last)
        def _():
            copy("dn", i).wait_recv()
            part[i] += dn_in[i].astype(F32)

        out_ref[place] = part[i].astype(BF16)

    @pl.when(works_on_pair(z, chips))
    def _():
        lax.fori_loop(0, 2 * TILES_DEV, finish, None)

    def drain(i, _):
        copy("ex", i).wait_send()

        @pl.when(i >= TILES_DEV * chips - up_count)
        def _():
            copy("up", i).wait_send()

        @pl.when(i < dn_count)
        def _():
            copy("dn", i).wait_send()

    lax.fori_loop(0, TILES_DEV * chips, drain, None)


def merge(table, pieces, parent_u, parent_v):
    fronts = lax.axis_size("front")
    chips = fronts // 2
    chunks = chips * TILES_DEV
    tile = (chunks, B, B)
    return pl.pallas_call(
        functools.partial(merge_kernel, chips),
        out_shape=jax.ShapeDtypeStruct((2 * TILES_DEV, B, B), BF16),
        in_specs=[
            pl.BlockSpec(memory_space=pltpu.SMEM),
            pl.BlockSpec(memory_space=pl.ANY),
            pl.BlockSpec(memory_space=pltpu.VMEM),
            pl.BlockSpec(memory_space=pltpu.VMEM),
        ],
        out_specs=pl.BlockSpec(memory_space=pltpu.VMEM),
        scratch_shapes=[
            pltpu.VMEM(pieces.shape, BF16),
            pltpu.SemaphoreType.DMA,
            pltpu.VMEM(tile, F32),
        ]
        + [pltpu.VMEM(tile, BF16)] * 6
        + [pltpu.SemaphoreType.DMA((chunks,))] * 6,
        compiler_params=pltpu.CompilerParams(
            collective_id=0, has_side_effects=True, vmem_limit_bytes=56 * 2**20
        ),
        name="merge",
    )(table, pieces, parent_u, parent_v)


def basis(y, work):
    eye = (
        lax.broadcasted_iota(jnp.int32, (R, R), 0) == lax.broadcasted_iota(jnp.int32, (R, R), 1)
    ).astype(F32)
    for t in range(2 * TILES_DEV):
        gram = dot_nt(y[t], y[t], HIGHEST)
        work[:, t, :] = jnp.concatenate((gram, eye), axis=1)
    rows = [work[i] for i in range(R)]
    for j in range(R):
        row = rows[j]
        pivot = jnp.broadcast_to(row[:, j : j + 1], row.shape)
        inverse = lax.rsqrt(pivot)
        scaled = row * (inverse * inverse)
        for i in range(j + 1, R):
            rows[i] = rows[i] - row[:, i : i + 1] * scaled
        work[j] = row * inverse
    return [
        dot_nn(work[:, t, :][:, R:], y[t], HIGHEST).astype(BF16) for t in range(2 * TILES_DEV)
    ]


def compress_kernel(m_ref, sketch_ref, w_ref, work):
    tiles = range(2 * TILES_DEV)
    sketch_t = sketch_ref[...]
    y = [dot_nt(sketch_t, m_ref[t]) for t in tiles]
    q = basis(y, work)
    mid = [dot_nn(q[t], m_ref[t]).astype(BF16) for t in tiles]
    y = [dot_nt(mid[t], m_ref[t]) for t in tiles]
    q = basis(y, work)
    for t in tiles:
        w_ref[t] = dot_nn(q[t], m_ref[t]).astype(BF16)


def compress(merged, sketch):
    return pl.pallas_call(
        compress_kernel,
        out_shape=jax.ShapeDtypeStruct((2 * TILES_DEV, R, B), BF16),
        in_specs=[pl.BlockSpec(memory_space=pltpu.VMEM)] * 2,
        out_specs=pl.BlockSpec(memory_space=pltpu.VMEM),
        scratch_shapes=[pltpu.VMEM((R, 2 * TILES_DEV, 2 * R), F32)],
        compiler_params=pltpu.CompilerParams(vmem_limit_bytes=32 * 2**20),
        name="compress",
    )(merged, sketch)


def couple_kernel(
    ranks, chips, found_ref, pivot_ref, coeff_ref, cores_ref,
    w, pivoted, gathered, give_send, give_recv, send, recv,
):
    me = lax.axis_index("tile")
    f = lax.axis_index("front")
    z = lax.div(f, 2)
    half = lax.rem(z, 2)
    partner = f + 2 - 4 * half
    worker = works_on_pair(z, chips)
    barrier = pltpu.get_barrier_semaphore()
    pl.semaphore_signal(barrier, inc=1, device_id={"front": partner}, device_id_type=MESH)
    for d in range(1, ranks):
        peer = lax.rem(me + d, ranks)
        pl.semaphore_signal(barrier, inc=1, device_id={"tile": peer}, device_id_type=MESH)
    pl.semaphore_wait(barrier, ranks)

    def give(s):
        return pltpu.make_async_remote_copy(
            src_ref=found_ref.at[(1 - half) * TILES_DEV + s], dst_ref=w.at[s],
            send_sem=give_send.at[s], recv_sem=give_recv.at[s],
            device_id={"front": partner}, device_id_type=MESH,
        )

    def copy(d, s):
        return pltpu.make_async_remote_copy(
            src_ref=pivoted.at[s], dst_ref=gathered.at[d - 1, s],
            send_sem=send.at[d - 1, s], recv_sem=recv.at[d - 1, s],
            device_id={"tile": lax.rem(me + d, ranks)}, device_id_type=MESH,
        )

    @pl.when(worker)
    def _():
        for s in range(TILES_DEV):
            give(s).start()
        for s in range(TILES_DEV):
            w[s] = found_ref[half * TILES_DEV + s]

    for s in range(TILES_DEV):
        @pl.when(jnp.logical_not(worker))
        def _():
            give(s).wait_recv()

        pivoted[s] = dot_nt(w[s], pivot_ref[...]).astype(BF16)
        for d in range(1, ranks):
            copy(d, s).start()

    wide = TILES_DEV * R
    own = w[...].reshape(wide, B)

    def place(source, block):
        cores_ref[:, pl.ds(pl.multiple_of(source * wide, wide), wide)] = dot_nt(
            own, block.reshape(wide, B)
        )

    place(me, pivoted[...])
    coeff_ref[...] = own.astype(F32).T.astype(BF16)
    for d in range(1, ranks):
        for s in range(TILES_DEV):
            copy(d, s).wait_recv()
        place(lax.rem(me + ranks - d, ranks), gathered[d - 1])
    for d in range(1, ranks):
        for s in range(TILES_DEV):
            copy(d, s).wait_send()

    @pl.when(worker)
    def _():
        for s in range(TILES_DEV):
            give(s).wait_send()


def couple(found, pivot_inverse):
    ranks = lax.axis_size("tile")
    chips = lax.axis_size("front") // 2
    wide = TILES_DEV * R
    return pl.pallas_call(
        functools.partial(couple_kernel, ranks, chips),
        out_shape=(
            jax.ShapeDtypeStruct((B, wide), BF16),
            jax.ShapeDtypeStruct((wide, ranks * wide), F32),
        ),
        in_specs=[pl.BlockSpec(memory_space=pltpu.VMEM)] * 2,
        out_specs=[pl.BlockSpec(memory_space=pltpu.VMEM)] * 2,
        scratch_shapes=[
            pltpu.VMEM((TILES_DEV, R, B), BF16),
            pltpu.VMEM((TILES_DEV, R, B), BF16),
            pltpu.VMEM((ranks - 1, TILES_DEV, R, B), BF16),
            pltpu.SemaphoreType.DMA((TILES_DEV,)),
            pltpu.SemaphoreType.DMA((TILES_DEV,)),
            pltpu.SemaphoreType.DMA((ranks - 1, TILES_DEV)),
            pltpu.SemaphoreType.DMA((ranks - 1, TILES_DEV)),
        ],
        compiler_params=pltpu.CompilerParams(
            collective_id=1, has_side_effects=True, vmem_limit_bytes=32 * 2**20
        ),
        name="couple",
    )(found, pivot_inverse)


def shards(pieces, dest_front, dest_slot, parent_u, parent_v, sketch, pivot_inverse):
    fronts = lax.axis_size("front")
    count = pieces.shape[0]
    ids = jnp.arange(count, dtype=jnp.int32)
    front_ids = dest_front[:, 0]
    prior = jnp.sum(
        ((front_ids[:, None] == front_ids[None, :]) & (ids[None, :] < ids[:, None])).astype(
            jnp.int32
        ),
        axis=1,
    )
    places = front_ids * SLOTS + prior
    hit = places[:, None] == jnp.arange(fronts * SLOTS, dtype=jnp.int32)[None, :]
    code = (ids * 8 + dest_slot - TILES_DEV)[:, None]
    table = jnp.sum(jnp.where(hit, code, 0), axis=0) + TILES_DEV
    merged = merge(table, pieces, parent_u, parent_v)
    return couple(compress(merged, sketch.T), pivot_inverse)


def solution(mesh):
    return jax.shard_map(
        shards,
        mesh=mesh,
        in_specs=(
            P(("front", "tile"), None, None),
            P(("front", "tile"), None),
            P(("front", "tile")),
            P("front", "tile"),
            P("front", "tile"),
            P(),
            P("front", None),
        ),
        out_specs=(P("front", "tile"), P(("front", "tile"), None)),
        check_vma=False,
    )
```

```python
import functools

import jax
import jax.numpy as jnp
from jax import lax
from jax.experimental import pallas as pl
from jax.experimental.pallas import tpu as pltpu
from jax.sharding import PartitionSpec as P

B = 256
R = 64
TILES_DEV = 4
CAP = 9
PAIRS = (CAP + 1) // 2
SLOTS = 2 * PAIRS
MESH = pl.DeviceIdType.MESH
F32 = jnp.float32
BF16 = jnp.bfloat16
HIGHEST = lax.Precision.HIGHEST


def dot_nt(a, b, precision=None):
    return lax.dot_general(
        a, b, (((1,), (1,)), ((), ())), precision=precision, preferred_element_type=F32
    )


def dot_nn(a, b, precision=None):
    return lax.dot_general(
        a, b, (((1,), (0,)), ((), ())), precision=precision, preferred_element_type=F32
    )


def merge_kernel(
    chips, table_ref, pieces_hbm, pu_ref, pv_ref, out_ref, pieces_ref, load_sem,
    part, ex_out, ex_in, up_out, up_in, dn_out, dn_in,
    ex_send, ex_recv, up_send, up_recv, dn_send, dn_recv,
):
    f = lax.axis_index("front")
    z = lax.div(f, 2)
    c = lax.rem(f, 2)
    sibling = 2 * z + 1 - c
    above = lax.rem(f + 2, 2 * chips)
    below = lax.rem(f + 2 * chips - 2, 2 * chips)
    last = chips - 1

    load = pltpu.make_async_copy(pieces_hbm, pieces_ref, load_sem)
    load.start()
    barrier = pltpu.get_barrier_semaphore()
    pl.semaphore_signal(barrier, inc=1, device_id={"front": sibling}, device_id_type=MESH)

    @pl.when(z > 0)
    def _():
        pl.semaphore_signal(barrier, inc=1, device_id={"front": below}, device_id_type=MESH)

    @pl.when(z < last)
    def _():
        pl.semaphore_signal(barrier, inc=1, device_id={"front": above}, device_id_type=MESH)

    pl.semaphore_wait(barrier, 1 + (z > 0).astype(jnp.int32) + (z < last).astype(jnp.int32))

    load.wait()

    def copy(kind, i):
        src, dst, send, recv, peer = {
            "ex": (ex_out, ex_in, ex_send, ex_recv, sibling),
            "up": (up_out, up_in, up_send, up_recv, above),
            "dn": (dn_out, dn_in, dn_send, dn_recv, below),
        }[kind]
        return pltpu.make_async_remote_copy(
            src_ref=src.at[i], dst_ref=dst.at[i], send_sem=send.at[i], recv_sem=recv.at[i],
            device_id={"front": peer}, device_id_type=MESH,
        )

    lane = lax.broadcasted_iota(jnp.int32, (1, 2 * R), 1)

    def partial(e):
        lefts, rights, owners = [], [], []
        for pair in range(PAIRS):
            first = table_ref[e * SLOTS + 2 * pair]
            second = table_ref[e * SLOTS + 2 * pair + 1]
            a = pieces_ref[lax.div(first, 8)]
            b = pieces_ref[lax.div(second, 8)]
            lefts.append(jnp.concatenate((a[:, :R], b[:, :R]), axis=1))
            rights.append(jnp.concatenate((a[:, R:], b[:, R:]), axis=1))
            owners.append(jnp.where(lane < R, lax.rem(first, 8), lax.rem(second, 8)))
        left = jnp.concatenate(lefts, axis=1)
        right = jnp.concatenate(rights, axis=1)
        owner = jnp.concatenate(owners, axis=1)
        masked = [
            left * jnp.where(owner == s, 1.0, 0.0).astype(BF16) for s in range(TILES_DEV)
        ]
        product = dot_nt(jnp.concatenate(masked, axis=0), right)
        return [product[s * B : (s + 1) * B] for s in range(TILES_DEV)]

    def flow(kind, t, s, incoming):
        i = t * TILES_DEV + s
        copy("ex", i).wait_recv()
        total = part[i] + ex_in[i].astype(F32)
        out = up_out if kind == "up" else dn_out
        if incoming:
            copy(kind, i).wait_recv()
            total = total + (up_in if kind == "up" else dn_in)[i].astype(F32)
        out[i] = total.astype(BF16)
        copy(kind, i).start()

    def end_flows(k):
        @pl.when(z == 0)
        def _():
            lax.fori_loop(0, TILES_DEV, lambda s, _: flow("up", last - k, s, False), None)

        @pl.when(z == last)
        def _():
            lax.fori_loop(0, TILES_DEV, lambda s, _: flow("dn", k, s, False), None)

    def compute(k, _):
        t = jnp.where(2 * z < chips, last - k, k)
        for s, total in enumerate(partial(2 * t + 1 - c)):
            ex_out[t * TILES_DEV + s] = total.astype(BF16)
            copy("ex", t * TILES_DEV + s).start()
        for s, total in enumerate(partial(2 * t + c)):
            part[t * TILES_DEV + s] = total

        @pl.when(k < last)
        def _():
            end_flows(k)

    lax.fori_loop(0, chips, compute, None)

    for s in range(TILES_DEV):
        cols = slice(s * R, (s + 1) * R)
        part[z * TILES_DEV + s] += dot_nt(pu_ref[:, cols], pv_ref[:, cols])

    def tick(n, _):
        up_n = n - z
        dn_n = n - (last - z)

        @pl.when((up_n >= 0) & (up_n < TILES_DEV * (last - z)))
        def _():
            flow("up", last - lax.div(up_n, TILES_DEV), lax.rem(up_n, TILES_DEV), True)

        @pl.when((dn_n >= 0) & (dn_n < TILES_DEV * z))
        def _():
            flow("dn", lax.div(dn_n, TILES_DEV), lax.rem(dn_n, TILES_DEV), True)

    @pl.when((z > 0) & (z < last))
    def _():
        lax.fori_loop(0, TILES_DEV * last + last, tick, None)

    def finish(s, _):
        i = z * TILES_DEV + s
        copy("ex", i).wait_recv()
        part[i] += ex_in[i].astype(F32)

        @pl.when(z > 0)
        def _():
            copy("up", i).wait_recv()
            part[i] += up_in[i].astype(F32)

        @pl.when(z < last)
        def _():
            copy("dn", i).wait_recv()
            part[i] += dn_in[i].astype(F32)

        out_ref[s] = part[i].astype(BF16)

    lax.fori_loop(0, TILES_DEV, finish, None)

    def drain(i, _):
        copy("ex", i).wait_send()

        @pl.when(i >= TILES_DEV * (z + 1))
        def _():
            copy("up", i).wait_send()

        @pl.when(i < TILES_DEV * z)
        def _():
            copy("dn", i).wait_send()

    lax.fori_loop(0, TILES_DEV * chips, drain, None)


def merge(table, pieces, parent_u, parent_v):
    fronts = lax.axis_size("front")
    chips = fronts // 2
    chunks = chips * TILES_DEV
    tile = (chunks, B, B)
    return pl.pallas_call(
        functools.partial(merge_kernel, chips),
        out_shape=jax.ShapeDtypeStruct((TILES_DEV, B, B), BF16),
        in_specs=[
            pl.BlockSpec(memory_space=pltpu.SMEM),
            pl.BlockSpec(memory_space=pl.ANY),
            pl.BlockSpec(memory_space=pltpu.VMEM),
            pl.BlockSpec(memory_space=pltpu.VMEM),
        ],
        out_specs=pl.BlockSpec(memory_space=pltpu.VMEM),
        scratch_shapes=[
            pltpu.VMEM(pieces.shape, BF16),
            pltpu.SemaphoreType.DMA,
            pltpu.VMEM(tile, F32),
        ]
        + [pltpu.VMEM(tile, BF16)] * 6
        + [pltpu.SemaphoreType.DMA((chunks,))] * 6,
        compiler_params=pltpu.CompilerParams(
            collective_id=0, has_side_effects=True, vmem_limit_bytes=56 * 2**20
        ),
        name="merge",
    )(table, pieces, parent_u, parent_v)


def basis(y, work):
    eye = (
        lax.broadcasted_iota(jnp.int32, (R, R), 0) == lax.broadcasted_iota(jnp.int32, (R, R), 1)
    ).astype(F32)
    for t in range(TILES_DEV):
        gram = dot_nt(y[t], y[t], HIGHEST)
        work[:, t, :] = jnp.concatenate((gram, eye), axis=1)
    rows = [work[i] for i in range(R)]
    for j in range(R):
        row = rows[j]
        pivot = jnp.broadcast_to(row[:, j : j + 1], row.shape)
        inverse = lax.rsqrt(pivot)
        scaled = row * (inverse * inverse)
        for i in range(j + 1, R):
            rows[i] = rows[i] - row[:, i : i + 1] * scaled
        work[j] = row * inverse
    return [
        dot_nn(work[:, t, :][:, R:], y[t], HIGHEST).astype(BF16) for t in range(TILES_DEV)
    ]


def compress_kernel(m_ref, sketch_ref, pivot_ref, w_ref, coeff_ref, pivoted_ref, work):
    tiles = range(TILES_DEV)
    work[...] = jnp.ones_like(work)
    sketch_t = sketch_ref[...]
    y = [dot_nt(sketch_t, m_ref[t]) for t in tiles]
    q = basis(y, work)
    mid = [dot_nn(q[t], m_ref[t]).astype(BF16) for t in tiles]
    y = [dot_nt(mid[t], m_ref[t]) for t in tiles]
    q = basis(y, work)
    w = jnp.concatenate([dot_nn(q[t], m_ref[t]) for t in tiles], axis=0)
    w_half = w.astype(BF16)
    w_ref[...] = w_half
    pivoted_ref[...] = dot_nt(w_half, pivot_ref[...]).astype(BF16)
    coeff_ref[...] = w.T.astype(BF16)


def compress(merged, sketch, pivot_inverse):
    wide = TILES_DEV * R
    return pl.pallas_call(
        compress_kernel,
        out_shape=(
            jax.ShapeDtypeStruct((wide, B), BF16),
            jax.ShapeDtypeStruct((B, wide), BF16),
            jax.ShapeDtypeStruct((wide, B), BF16),
        ),
        in_specs=[pl.BlockSpec(memory_space=pltpu.VMEM)] * 3,
        out_specs=[pl.BlockSpec(memory_space=pltpu.VMEM)] * 3,
        scratch_shapes=[pltpu.VMEM((R, 8, 2 * R), F32)],
        compiler_params=pltpu.CompilerParams(vmem_limit_bytes=32 * 2**20),
        name="compress",
    )(merged, sketch, pivot_inverse)


def couple_kernel(ranks, w_ref, p_ref, cores_ref, gathered, send, recv):
    me = lax.axis_index("tile")
    barrier = pltpu.get_barrier_semaphore()
    for d in range(1, ranks):
        peer = lax.rem(me + d, ranks)
        pl.semaphore_signal(barrier, inc=1, device_id={"tile": peer}, device_id_type=MESH)
    pl.semaphore_wait(barrier, ranks - 1)

    def copy(d):
        return pltpu.make_async_remote_copy(
            src_ref=p_ref, dst_ref=gathered.at[d - 1], send_sem=send.at[d - 1],
            recv_sem=recv.at[d - 1], device_id={"tile": lax.rem(me + d, ranks)},
            device_id_type=MESH,
        )

    for d in range(1, ranks):
        copy(d).start()
    wide = TILES_DEV * R

    def place(source, block):
        cores_ref[:, pl.ds(pl.multiple_of(source * wide, wide), wide)] = dot_nt(w_ref[...], block)

    place(me, p_ref[...])
    for d in range(1, ranks):
        copy(d).wait_recv()
        place(lax.rem(me + ranks - d, ranks), gathered[d - 1])
    for d in range(1, ranks):
        copy(d).wait_send()


def couple(w, pivoted):
    ranks = lax.axis_size("tile")
    wide = TILES_DEV * R
    return pl.pallas_call(
        functools.partial(couple_kernel, ranks),
        out_shape=jax.ShapeDtypeStruct((wide, ranks * wide), F32),
        in_specs=[pl.BlockSpec(memory_space=pltpu.VMEM)] * 2,
        out_specs=pl.BlockSpec(memory_space=pltpu.VMEM),
        scratch_shapes=[
            pltpu.VMEM((ranks - 1, wide, B), BF16),
            pltpu.SemaphoreType.DMA((ranks - 1,)),
            pltpu.SemaphoreType.DMA((ranks - 1,)),
        ],
        compiler_params=pltpu.CompilerParams(
            collective_id=1, has_side_effects=True, vmem_limit_bytes=32 * 2**20
        ),
        name="couple",
    )(w, pivoted)


def shards(pieces, dest_front, dest_slot, parent_u, parent_v, sketch, pivot_inverse):
    fronts = lax.axis_size("front")
    count = pieces.shape[0]
    ids = jnp.arange(count, dtype=jnp.int32)
    front_ids = dest_front[:, 0]
    prior = jnp.sum(
        ((front_ids[:, None] == front_ids[None, :]) & (ids[None, :] < ids[:, None])).astype(
            jnp.int32
        ),
        axis=1,
    )
    places = front_ids * SLOTS + prior
    hit = places[:, None] == jnp.arange(fronts * SLOTS, dtype=jnp.int32)[None, :]
    code = (ids * 8 + dest_slot - TILES_DEV)[:, None]
    table = jnp.sum(jnp.where(hit, code, 0), axis=0) + TILES_DEV
    merged = merge(table, pieces, parent_u, parent_v)
    w, coeff, pivoted = compress(merged, sketch.T, pivot_inverse)
    return (coeff, couple(w, pivoted))


def solution(mesh):
    return jax.shard_map(
        shards,
        mesh=mesh,
        in_specs=(
            P(("front", "tile"), None, None),
            P(("front", "tile"), None),
            P(("front", "tile")),
            P("front", "tile"),
            P("front", "tile"),
            P(),
            P("front", None),
        ),
        out_specs=(P("front", "tile"), P(("front", "tile"), None)),
        check_vma=False,
    )
```
